256 devices in a mesh: row: 16 (over x, y), col: 16 (over z, core).
Axes of the slice: x: 4, y: 4, z: 8, core: 2. Of those that a mesh axis runs over, the one named last changes fastest.
Arguments:
- stiffness: bfloat16 [36864, 36864], P('row', 'col'), may hold values from -0.046875 to 0.046875
- self_stiffness: float32 [36864], P(('row', 'col')), may hold values from 1 to 2
- stress: float32 [36864, 256], P(('row', 'col')), may hold values from -0.5 to 0.5
- state: float32 [36864, 256], P(('row', 'col')), may hold values from 0 to 1
- plate_rate: float32 [36864], P(('row', 'col')), may hold values from 0.2 to 1
- stress_gain: float32 [36864], P(('row', 'col')), may hold values from 0.5 to 2
- heal_rate: float32 [36864], P(('row', 'col')), may hold values from 0.2 to 2
- ab_ratio: float32 [36864], P(('row', 'col')), may hold values from 0.5 to 2
- step: float32 [256], replicated, may hold values from 0.05 to 0.2
Outputs:
- stress_next: float32 [36864, 256], P(('row', 'col'))
- state_next: float32 [36864, 256], P(('row', 'col'))
- error_norm: float32 [256], replicated
The draws below stay inside these ranges and needn't reach their ends.
All inputs are finite; a program needn't handle non-finite values.
Results may differ from the reference program's by a relative error of at most 0.00085.
Values may be sent and summed in bfloat16 or wider, within the bound.
No kernel may reach another device: no remote copies, remote signals or barrier semaphores. Data moves between devices by JAX's collectives and lax.ppermute only.
A program may use at most 128 MiB of HBM per device.

```python
import math
import jax
import jax.numpy as jnp
from jax import lax

MEMBERS = 256
N = 36864


def spiked(entries, rng, source, target, blocks, factor):
    owner, partner = [(jnp.arange(entries.shape[position]) // (entries.shape[position] // blocks)).reshape([-1 if axis == position else 1 for axis in range(entries.ndim)]) for position in (source, target)]
    chosen = jax.random.permutation(rng, blocks)[partner]
    strong = (owner == chosen) | (owner == (partner + blocks // 2) % blocks)
    return jnp.where(strong, factor * entries, entries)


def shard_levels(stream_key, shape, cuts, low, top_value):
    factor_of = 1.0
    for position, parts in cuts:
        steps = jax.random.uniform(jax.random.fold_in(jax.random.fold_in(stream_key, 6), position), (parts,), jnp.float32, low / len(cuts), top_value / len(cuts))
        factor_of = factor_of * jnp.repeat(jnp.exp(steps), shape[position] // parts).reshape((-1,) + (1,) * (len(shape) - 1 - position))
    return factor_of


def noise_with(rng, shape, width, limit, cuts, heavy, held_as=jnp.bfloat16):
    result = width * jax.random.normal(rng, shape, jnp.float32)
    if cuts:
        result = result * shard_levels(rng, shape, cuts, -0.22, 0.18)
    return jnp.clip(spiked(result, jax.random.fold_in(rng, 3), *heavy), -limit, limit).astype(held_as)


def setup_inputs(seed: int = 0) -> dict:
    keys = jax.random.split(jax.random.key(seed), 10)
    return {
        "stiffness": noise_with(keys[0], (N, N), N ** -0.5, 0.046875, ((0, 16), (1, 16)), (1, 0, 16, 2.0)),
        "self_stiffness": jnp.clip(jnp.exp(math.log(2.0) - 0.6931472 * jax.random.uniform(keys[1], (N,), jnp.float32) ** shard_levels(keys[1], (N,), ((0, 256),), -0.2, 0.2)), 1.0, 2.0),
        "stress": jnp.clip(jax.random.uniform(keys[2], (N, MEMBERS), jnp.float32, -0.5, 0.5) * shard_levels(keys[2], (N, MEMBERS), ((0, 256),), -0.4, 0.0), -0.5, 0.5),
        "state": jnp.clip(1.0 * jax.random.uniform(keys[3], (N, MEMBERS), jnp.float32) ** shard_levels(keys[3], (N, MEMBERS), ((0, 256),), -0.2, 0.2), 0.0, 1.0),
        "plate_rate": jnp.clip(jnp.exp(math.log(1.0) - 1.609438 * jax.random.uniform(keys[4], (N,), jnp.float32) ** shard_levels(keys[4], (N,), ((0, 256),), -0.2, 0.2)), 0.2, 1.0),
        "stress_gain": jnp.clip(jnp.exp(math.log(2.0) - 1.3862944 * jax.random.uniform(keys[5], (N,), jnp.float32) ** shard_levels(keys[5], (N,), ((0, 256),), -0.2, 0.2)), 0.5, 2.0),
        "heal_rate": jnp.clip(jnp.exp(math.log(2.0) - 2.3025851 * jax.random.uniform(keys[6], (N,), jnp.float32) ** shard_levels(keys[6], (N,), ((0, 256),), -0.2, 0.2)), 0.2, 2.0),
        "ab_ratio": jnp.clip(jnp.exp(math.log(2.0) - 1.3862944 * jax.random.uniform(keys[7], (N,), jnp.float32) ** shard_levels(keys[7], (N,), ((0, 256),), -0.2, 0.2)), 0.5, 2.0),
        "step": jnp.clip(jnp.exp(jax.random.uniform(keys[8], (MEMBERS,), jnp.float32, math.log(0.05), math.log(0.2))), 0.05, 0.2),
    }


tolerance = 0.01
epsilon = 1e-06

def tendencies(stress_now, state_now, stiffness, self_stiffness, plate_rate, stress_gain, heal_rate, ab_ratio):
    slip_rate = 2.0 * jnp.sinh(stress_now) * jnp.exp(-state_now)
    deficit = slip_rate - plate_rate[:, None]
    coupled = jnp.dot(stiffness, deficit.astype(jnp.bfloat16), preferred_element_type=jnp.float32)
    stress_rate = stress_gain[:, None] * (-self_stiffness[:, None] * deficit - coupled)
    state_rate = heal_rate[:, None] * (jnp.exp(-ab_ratio[:, None] * state_now) - slip_rate)
    return (stress_rate, state_rate)

def reference(stiffness, self_stiffness, stress, state, plate_rate, stress_gain, heal_rate, ab_ratio, step):
    params = (stiffness, self_stiffness, plate_rate, stress_gain, heal_rate, ab_ratio)
    first_u, first_p = tendencies(stress, state, *params)
    full_step = step[None, :]
    second_u, second_p = tendencies(stress + full_step * first_u, state + full_step * first_p, *params)
    half_step = 0.5 * full_step
    stress_next = stress + half_step * (first_u + second_u)
    state_next = state + half_step * (first_p + second_p)
    depth = 0.5 + 1.5 * (jnp.arange(N, dtype=jnp.float32) + 0.5) / N
    squared = (depth[:, None] * half_step * (second_u - first_u)) ** 2 + (half_step * (second_p - first_p)) ** 2
    error_norm = jnp.sqrt(lax.optimization_barrier(jnp.sum(squared, axis=0)) / (2 * N) + epsilon) / tolerance
    return (stress_next, state_next, error_norm)
```

```python
import jax
import jax.numpy as jnp
from jax import lax
from jax.experimental import pallas as pl
from jax.experimental.pallas import tpu as pltpu
from jax.sharding import PartitionSpec as P

tolerance = 0.01
epsilon = 1e-06
BOTH = ("row", "col")


def friction(stress_now, state_now, plate_vel):
    slip_rate = 2.0 * jnp.sinh(stress_now) * jnp.exp(-state_now)
    return (slip_rate, slip_rate - plate_vel[:, None])


def rates_from(state_now, slip_rate, deficit, coupled, params):
    diag_stiff, plate_vel, gain_now, heal_now, ratio_now = params
    stress_rate = gain_now[:, None] * (-diag_stiff[:, None] * deficit - coupled)
    state_rate = heal_now[:, None] * (jnp.exp(-ratio_now[:, None] * state_now) - slip_rate)
    return (stress_rate, state_rate)


def half_product(stiff, segment, parity, received=None):
    half, _, owned, depth = stiff.shape
    members = segment.shape[1]

    def kernel(parity_ref, stiff_ref, segment_ref, *rest):
        out_ref = rest[-1]
        rows = stiff_ref[:, parity_ref[0]].reshape(half * owned, depth)
        product = jnp.dot(rows, segment_ref[...], preferred_element_type=jnp.float32)
        product = product.reshape(half, owned, members)
        if received is not None:
            product = product + rest[0][...].astype(jnp.float32)
        out_ref[...] = product.astype(jnp.bfloat16)

    operands = (parity, stiff, segment) + (() if received is None else (received,))
    vmem = pl.BlockSpec(memory_space=pltpu.VMEM)
    return pl.pallas_call(
        kernel,
        out_shape=jax.ShapeDtypeStruct((half, owned, members), jnp.bfloat16),
        in_specs=[pl.BlockSpec(memory_space=pltpu.SMEM)] + [vmem] * (len(operands) - 1),
        out_specs=vmem,
        compiler_params=pltpu.CompilerParams(vmem_limit_bytes=32 << 20),
        cost_estimate=pl.CostEstimate(
            flops=2 * half * owned * depth * members,
            bytes_accessed=2 * half * owned * depth,
            transcendentals=0,
        ),
    )(*operands)


def body(
    stiffness, self_stiffness, stress, state, plate_rate, stress_gain, heal_rate, ab_ratio, step
):
    owned, members = stress.shape
    side = lax.axis_size("row")
    layers = side // 2
    row_index = lax.axis_index("row")
    col_index = lax.axis_index("col")
    patch_total = owned * side * side
    params = (self_stiffness, plate_rate, stress_gain, heal_rate, ab_ratio)
    first_patch = (row_index * side + col_index) * owned

    everyone = range(side)
    spread = [(a * side + b, (a ^ b) * side + a) for a in everyone for b in everyone]
    plane_groups = [[(a ^ b) * side + a for b in everyone] for a in everyone]
    same_core = [[2 * z + core for z in range(layers)] for core in range(2)]
    swap = [(c, c ^ 1) for c in everyone]
    parity = col_index % 2
    mine = parity.astype(jnp.int32).reshape(1)
    theirs = 1 - mine
    stiff = stiffness.reshape(layers, 2, owned, side * owned)

    def coupling(sent_block):
        moved = lax.ppermute(sent_block, BOTH, spread)
        copies = jnp.broadcast_to(moved[None], (side, owned, members))
        segment = lax.all_to_all(
            copies, BOTH, 0, 0, axis_index_groups=plane_groups, tiled=True
        ).reshape(side * owned, members)
        away = half_product(stiff, segment, theirs)
        received = lax.ppermute(away, "col", swap)
        kept = half_product(stiff, segment, mine, received)
        terms = lax.all_to_all(kept, "col", 0, 0, axis_index_groups=same_core, tiled=True)
        return jnp.sum(terms.astype(jnp.float32), axis=0)

    def section(stress_now, state_now):
        slip_rate, deficit = friction(stress_now, state_now, params[1])
        coupled = coupling(deficit.astype(jnp.bfloat16))
        return rates_from(state_now, slip_rate, deficit, coupled, params)

    def total_over(values, axis):
        copies = jnp.broadcast_to(values[None], (side, members))
        return jnp.sum(lax.all_to_all(copies, axis, 0, 0, tiled=True), axis=0)

    full_step = step[None, :]
    first_u, first_p = section(stress, state)
    second_u, second_p = section(stress + full_step * first_u, state + full_step * first_p)
    half_step = 0.5 * full_step
    stress_next = stress + half_step * (first_u + second_u)
    state_next = state + half_step * (first_p + second_p)
    positions = first_patch + jnp.arange(owned, dtype=jnp.int32)
    depth = 0.5 + 1.5 * (positions.astype(jnp.float32) + 0.5) / patch_total
    squared = (depth[:, None] * half_step * (second_u - first_u)) ** 2 + (
        half_step * (second_p - first_p)
    ) ** 2
    partial_sums = jnp.sum(squared, axis=0)
    summed = total_over(total_over(partial_sums, "col"), "row")
    error_norm = jnp.sqrt(summed / (2 * patch_total) + epsilon) / tolerance
    return (stress_next, state_next, error_norm)


def solution(mesh):
    return jax.shard_map(
        body,
        mesh=mesh,
        in_specs=(
            P("row", "col"),
            P(("row", "col")),
            P(("row", "col"), None),
            P(("row", "col"), None),
            P(("row", "col")),
            P(("row", "col")),
            P(("row", "col")),
            P(("row", "col")),
            P(),
        ),
        out_specs=(P(("row", "col"), None), P(("row", "col"), None), P()),
        check_vma=False,
    )
```

```python
import jax
import jax.numpy as jnp
from jax import lax
from jax.experimental import pallas as pl
from jax.experimental.pallas import tpu as pltpu
from jax.sharding import PartitionSpec as P

tolerance = 0.01
epsilon = 1e-06
VMEM_LIMIT = 16 << 20
BOTH = ("row", "col")


def friction(stress_now, state_now, plate_vel):
    slip_rate = 2.0 * jnp.sinh(stress_now) * jnp.exp(-state_now)
    return (slip_rate, slip_rate - plate_vel[:, None])


def rates_from(state_now, slip_rate, deficit, coupled, params):
    diag_stiff, plate_vel, gain_now, heal_now, ratio_now = params
    stress_rate = gain_now[:, None] * (-diag_stiff[:, None] * deficit - coupled)
    state_rate = heal_now[:, None] * (jnp.exp(-ratio_now[:, None] * state_now) - slip_rate)
    return (stress_rate, state_rate)


def ring_distance(first, second, size):
    return min((first - second) % size, (second - first) % size)


def landing_rows(side, width):
    layers = side // 2
    table = []
    for a in range(side):
        far = sorted(
            range(side), key=lambda b: (-ring_distance(b // 2, a // 2, layers), a ^ b)
        )
        near = sorted(
            range(side),
            key=lambda r: (
                ring_distance(r // width, a // width, width)
                + ring_distance(r % width, a % width, width),
                a ^ r,
            ),
        )
        rows = dict(zip(far, near))
        table.append([rows[b] for b in range(side)])
    return table


def resident(stiff):
    def kernel(stiff_ref, out_ref, done):
        copy = pltpu.make_async_copy(stiff_ref, out_ref, done)
        copy.start()
        copy.wait()

    return pl.pallas_call(
        kernel,
        out_shape=jax.ShapeDtypeStruct(stiff.shape, stiff.dtype),
        in_specs=[pl.BlockSpec(memory_space=pltpu.HBM)],
        out_specs=pl.BlockSpec(memory_space=pltpu.VMEM),
        scratch_shapes=[pltpu.SemaphoreType.DMA],
        compiler_params=pltpu.CompilerParams(vmem_limit_bytes=16 << 20),
        cost_estimate=pl.CostEstimate(
            flops=0, bytes_accessed=4 * stiff.size, transcendentals=0
        ),
    )(stiff)


def half_product(stiff, segment, swapped, dtype):
    half, _, owned, depth = stiff.shape
    members = segment.shape[1]

    def kernel(stiff_ref, segment_ref, out_ref, kept_ref):
        core = (lax.axis_index("col") + swapped) % 2
        rows = stiff_ref[:, core].reshape(half * owned, depth)
        product = jnp.dot(rows, segment_ref[...], preferred_element_type=jnp.float32)
        out_ref[...] = product.reshape(half, owned, members).astype(dtype)

    vmem = pl.BlockSpec(memory_space=pltpu.VMEM)
    return pl.pallas_call(
        kernel,
        out_shape=(
            jax.ShapeDtypeStruct((half, owned, members), dtype),
            jax.ShapeDtypeStruct(stiff.shape, stiff.dtype),
        ),
        in_specs=[vmem, vmem],
        out_specs=(vmem, vmem),
        input_output_aliases={0: 1},
        compiler_params=pltpu.CompilerParams(vmem_limit_bytes=VMEM_LIMIT),
        cost_estimate=pl.CostEstimate(
            flops=2 * half * owned * depth * members,
            bytes_accessed=2 * half * owned * depth,
            transcendentals=0,
        ),
    )(stiff, segment)


def body(
    stiffness, self_stiffness, stress, state, plate_rate, stress_gain, heal_rate, ab_ratio, step
):
    owned, members = stress.shape
    side = lax.axis_size("row")
    layers = side // 2
    row_index = lax.axis_index("row")
    col_index = lax.axis_index("col")
    patch_total = owned * side * side
    params = (self_stiffness, plate_rate, stress_gain, heal_rate, ab_ratio)
    first_patch = (row_index * side + col_index) * owned

    everyone = range(side)
    rows = landing_rows(side, 4)
    spread = [(a * side + b, rows[a][b] * side + a) for a in everyone for b in everyone]
    plane_groups = [[rows[a][b] * side + a for b in everyone] for a in everyone]
    same_core = [[2 * z + core for z in range(layers)] for core in range(2)]
    swap = [(c, c ^ 1) for c in everyone]
    stiff = stiffness.reshape(layers, 2, owned, side * owned)
    positions = first_patch + jnp.arange(owned, dtype=jnp.int32)
    depth = 0.5 + 1.5 * (positions.astype(jnp.float32) + 0.5) / patch_total

    def coupling(sent_block, stiff, late):
        moved = lax.ppermute(sent_block, BOTH, spread)
        copies = jnp.broadcast_to(moved[None], (side, owned, members))
        copies, stiff, late = lax.optimization_barrier((copies, stiff, late))
        segment = lax.all_to_all(
            copies, BOTH, 0, 0, axis_index_groups=plane_groups, tiled=True
        ).reshape(side * owned, members)
        segment, stiff, late = lax.optimization_barrier((segment, stiff, late))
        away, stiff = half_product(stiff, segment, 1, jnp.bfloat16)
        received = lax.ppermute(away, "col", swap)
        own, stiff = half_product(stiff, segment, 0, jnp.float32)
        kept = (own + received.astype(jnp.float32)).astype(jnp.bfloat16)
        kept, stiff, late = lax.optimization_barrier((kept, stiff, late))
        terms = lax.all_to_all(kept, "col", 0, 0, axis_index_groups=same_core, tiled=True)
        terms, stiff, late = lax.optimization_barrier((terms, stiff, late))
        return jnp.sum(terms.astype(jnp.float32), axis=0), stiff, late

    def section(stress_now, state_now, stiff, late):
        params = late[:5]
        slip_rate, deficit = friction(stress_now, state_now, plate_rate)
        late = (*late, stress_now, state_now)
        coupled, stiff, late = coupling(deficit.astype(jnp.bfloat16), stiff, late)
        *late, stress_now, state_now = late
        slip_rate, deficit = friction(stress_now, state_now, late[1])
        tendencies = rates_from(state_now, slip_rate, deficit, coupled, tuple(late[:5]))
        return tendencies, stiff, tuple(late)

    def total_over(values, axis):
        copies = jnp.broadcast_to(values[None], (side, members))
        return jnp.sum(lax.all_to_all(copies, axis, 0, 0, tiled=True), axis=0)

    depth, stiff = lax.optimization_barrier((depth, stiff))
    late = (*params, step, depth, stress, state)
    (first_u, first_p), stiff, late = section(stress, state, resident(stiff), late)
    *_, step, depth, stress, state = late
    full_step = step[None, :]
    late = (*late, first_u, first_p)
    (second_u, second_p), stiff, late = section(
        stress + full_step * first_u, state + full_step * first_p, stiff, late
    )
    *_, step, depth, stress, state, first_u, first_p = late
    half_step = 0.5 * step[None, :]
    stress_next = stress + half_step * (first_u + second_u)
    state_next = state + half_step * (first_p + second_p)
    squared = (depth[:, None] * half_step * (second_u - first_u)) ** 2 + (
        half_step * (second_p - first_p)
    ) ** 2
    partial_sums = jnp.sum(squared, axis=0)
    summed = total_over(total_over(partial_sums, "col"), "row")
    error_norm = jnp.sqrt(summed / (2 * patch_total) + epsilon) / tolerance
    return (stress_next, state_next, error_norm)


def solution(mesh):
    return jax.shard_map(
        body,
        mesh=mesh,
        in_specs=(
            P("row", "col"),
            P(("row", "col")),
            P(("row", "col"), None),
            P(("row", "col"), None),
            P(("row", "col")),
            P(("row", "col")),
            P(("row", "col")),
            P(("row", "col")),
            P(),
        ),
        out_specs=(P(("row", "col"), None), P(("row", "col"), None), P()),
        check_vma=False,
    )
```

```python
import jax
import jax.numpy as jnp
from jax import lax
from jax.experimental import pallas as pl
from jax.experimental.pallas import tpu as pltpu
from jax.sharding import PartitionSpec as P

tolerance = 0.01
epsilon = 1e-06
VMEM_LIMIT = 16 << 20
BOTH = ("row", "col")


def friction(stress_now, state_now, plate_vel):
    slip_rate = 2.0 * jnp.sinh(stress_now) * jnp.exp(-state_now)
    return (slip_rate, slip_rate - plate_vel[:, None])


def rates_from(state_now, slip_rate, deficit, coupled, params):
    diag_stiff, plate_vel, gain_now, heal_now, ratio_now = params
    stress_rate = gain_now[:, None] * (-diag_stiff[:, None] * deficit - coupled)
    state_rate = heal_now[:, None] * (jnp.exp(-ratio_now[:, None] * state_now) - slip_rate)
    return (stress_rate, state_rate)


def ring_distance(first, second, size):
    return min((first - second) % size, (second - first) % size)


def landing_rows(side, width):
    layers = side // 2
    table = []
    for a in range(side):
        far = sorted(
            range(side), key=lambda b: (-ring_distance(b // 2, a // 2, layers), a ^ b)
        )
        near = sorted(
            range(side),
            key=lambda r: (
                ring_distance(r // width, a // width, width)
                + ring_distance(r % width, a % width, width),
                a ^ r,
            ),
        )
        rows = dict(zip(far, near))
        table.append([rows[b] for b in range(side)])
    return table


def resident(stiff):
    def kernel(stiff_ref, out_ref, done):
        copy = pltpu.make_async_copy(stiff_ref, out_ref, done)
        copy.start()
        copy.wait()

    return pl.pallas_call(
        kernel,
        out_shape=jax.ShapeDtypeStruct(stiff.shape, stiff.dtype),
        in_specs=[pl.BlockSpec(memory_space=pltpu.HBM)],
        out_specs=pl.BlockSpec(memory_space=pltpu.VMEM),
        scratch_shapes=[pltpu.SemaphoreType.DMA],
        compiler_params=pltpu.CompilerParams(vmem_limit_bytes=16 << 20),
        cost_estimate=pl.CostEstimate(
            flops=0, bytes_accessed=4 * stiff.size, transcendentals=0
        ),
    )(stiff)


def class_product(stiff, segment, other_layer, other_core, dtype):
    quarter, _, _, owned, depth = stiff.shape
    members = segment.shape[1]

    def kernel(stiff_ref, segment_ref, out_ref, kept_ref):
        col = lax.axis_index("col")
        layer_parity = (col // 2 + other_layer) % 2
        core = (col + other_core) % 2
        rows = stiff_ref[:, layer_parity, core].reshape(quarter * owned, depth)
        product = jnp.dot(rows, segment_ref[...], preferred_element_type=jnp.float32)
        out_ref[...] = product.reshape(quarter, owned, members).astype(dtype)

    vmem = pl.BlockSpec(memory_space=pltpu.VMEM)
    return pl.pallas_call(
        kernel,
        out_shape=(
            jax.ShapeDtypeStruct((quarter, owned, members), dtype),
            jax.ShapeDtypeStruct(stiff.shape, stiff.dtype),
        ),
        in_specs=[vmem, vmem],
        out_specs=(vmem, vmem),
        input_output_aliases={0: 1},
        compiler_params=pltpu.CompilerParams(vmem_limit_bytes=VMEM_LIMIT),
        cost_estimate=pl.CostEstimate(
            flops=2 * quarter * owned * depth * members,
            bytes_accessed=2 * quarter * owned * depth,
            transcendentals=0,
        ),
    )(stiff, segment)


def body(
    stiffness, self_stiffness, stress, state, plate_rate, stress_gain, heal_rate, ab_ratio, step
):
    owned, members = stress.shape
    side = lax.axis_size("row")
    layers = side // 2
    row_index = lax.axis_index("row")
    col_index = lax.axis_index("col")
    patch_total = owned * side * side
    params = (self_stiffness, plate_rate, stress_gain, heal_rate, ab_ratio)
    first_patch = (row_index * side + col_index) * owned

    everyone = range(side)
    rows = landing_rows(side, 4)
    spread = [(a * side + b, rows[a][b] * side + a) for a in everyone for b in everyone]
    plane_groups = [[rows[a][b] * side + a for b in everyone] for a in everyone]
    same_class = [
        [2 * z + core for z in range(parity, layers, 2)]
        for core in range(2)
        for parity in range(2)
    ]
    swap = [(c, c ^ 1) for c in everyone]
    beside = []
    for c in everyone:
        z, core = c // 2, c % 2
        ahead = (z + core) % 2 == 0
        beside.append((c, 2 * ((z + (1 if ahead else -1)) % layers) + core))
    stiff = stiffness.reshape(layers // 2, 2, 2, owned, side * owned)
    positions = first_patch + jnp.arange(owned, dtype=jnp.int32)
    depth = 0.5 + 1.5 * (positions.astype(jnp.float32) + 0.5) / patch_total

    def coupling(sent_block, stiff, late):
        moved = lax.ppermute(sent_block, BOTH, spread)
        copies = jnp.broadcast_to(moved[None], (side, owned, members))
        copies, stiff, late = lax.optimization_barrier((copies, stiff, late))
        segment = lax.all_to_all(
            copies, BOTH, 0, 0, axis_index_groups=plane_groups, tiled=True
        ).reshape(side * owned, members)
        segment, stiff, late = lax.optimization_barrier((segment, stiff, late))
        part, stiff = class_product(stiff, segment, 1, 1, jnp.float32)
        received = lax.ppermute(part, "col", swap)
        own, stiff = class_product(stiff, segment, 1, 0, jnp.float32)
        onward = (own + received.astype(jnp.float32)).astype(jnp.bfloat16)
        arrived = lax.ppermute(onward, "col", beside)
        part, stiff = class_product(stiff, segment, 0, 1, jnp.float32)
        received = lax.ppermute(part, "col", swap)
        own, stiff = class_product(stiff, segment, 0, 0, jnp.float32)
        kept = (own + received + arrived.astype(jnp.float32)).astype(jnp.bfloat16)
        kept, stiff, late = lax.optimization_barrier((kept, stiff, late))
        terms = lax.all_to_all(kept, "col", 0, 0, axis_index_groups=same_class, tiled=True)
        terms, stiff, late = lax.optimization_barrier((terms, stiff, late))
        return jnp.sum(terms.astype(jnp.float32), axis=0), stiff, late

    def section(stress_now, state_now, stiff, late):
        params = late[:5]
        slip_rate, deficit = friction(stress_now, state_now, plate_rate)
        late = (*late, stress_now, state_now)
        coupled, stiff, late = coupling(deficit.astype(jnp.bfloat16), stiff, late)
        *late, stress_now, state_now = late
        slip_rate, deficit = friction(stress_now, state_now, late[1])
        tendencies = rates_from(state_now, slip_rate, deficit, coupled, tuple(late[:5]))
        return tendencies, stiff, tuple(late)

    def total_over(values, axis):
        copies = jnp.broadcast_to(values[None], (side, members))
        return jnp.sum(lax.all_to_all(copies, axis, 0, 0, tiled=True), axis=0)

    depth, stiff = lax.optimization_barrier((depth, stiff))
    late = (*params, step, depth, stress, state)
    (first_u, first_p), stiff, late = section(stress, state, resident(stiff), late)
    *_, step, depth, stress, state = late
    full_step = step[None, :]
    late = (*late, first_u, first_p)
    (second_u, second_p), stiff, late = section(
        stress + full_step * first_u, state + full_step * first_p, stiff, late
    )
    *_, step, depth, stress, state, first_u, first_p = late
    half_step = 0.5 * step[None, :]
    stress_next = stress + half_step * (first_u + second_u)
    state_next = state + half_step * (first_p + second_p)
    squared = (depth[:, None] * half_step * (second_u - first_u)) ** 2 + (
        half_step * (second_p - first_p)
    ) ** 2
    partial_sums = jnp.sum(squared, axis=0)
    summed = total_over(total_over(partial_sums, "col"), "row")
    error_norm = jnp.sqrt(summed / (2 * patch_total) + epsilon) / tolerance
    return (stress_next, state_next, error_norm)


def solution(mesh):
    return jax.shard_map(
        body,
        mesh=mesh,
        in_specs=(
            P("row", "col"),
            P(("row", "col")),
            P(("row", "col"), None),
            P(("row", "col"), None),
            P(("row", "col")),
            P(("row", "col")),
            P(("row", "col")),
            P(("row", "col")),
            P(),
        ),
        out_specs=(P(("row", "col"), None), P(("row", "col"), None), P()),
        check_vma=False,
    )
```

```python
import jax
import jax.numpy as jnp
from jax import lax
from jax.experimental import pallas as pl
from jax.experimental.pallas import tpu as pltpu
from jax.sharding import PartitionSpec as P

tolerance = 0.01
epsilon = 1e-06
VMEM_LIMIT = 16 << 20
BOTH = ("row", "col")


def friction(stress_now, state_now, plate_vel):
    slip_rate = 2.0 * jnp.sinh(stress_now) * jnp.exp(-state_now)
    return (slip_rate, slip_rate - plate_vel[:, None])


def rates_from(state_now, slip_rate, deficit, coupled, params):
    diag_stiff, plate_vel, gain_now, heal_now, ratio_now = params
    stress_rate = gain_now[:, None] * (-diag_stiff[:, None] * deficit - coupled)
    state_rate = heal_now[:, None] * (jnp.exp(-ratio_now[:, None] * state_now) - slip_rate)
    return (stress_rate, state_rate)


def ring_distance(first, second, size):
    return min((first - second) % size, (second - first) % size)


def landing_rows(side, width):
    layers = side // 2
    table = []
    for a in range(side):
        far = sorted(
            range(side), key=lambda b: (-ring_distance(b // 2, a // 2, layers), a ^ b)
        )
        near = sorted(
            range(side),
            key=lambda r: (
                ring_distance(r // width, a // width, width)
                + ring_distance(r % width, a % width, width),
                a ^ r,
            ),
        )
        rows = dict(zip(far, near))
        table.append([rows[b] for b in range(side)])
    return table


def resident(stiff):
    def kernel(stiff_ref, out_ref, done):
        copy = pltpu.make_async_copy(stiff_ref, out_ref, done)
        copy.start()
        copy.wait()

    return pl.pallas_call(
        kernel,
        out_shape=jax.ShapeDtypeStruct(stiff.shape, stiff.dtype),
        in_specs=[pl.BlockSpec(memory_space=pltpu.HBM)],
        out_specs=pl.BlockSpec(memory_space=pltpu.VMEM),
        scratch_shapes=[pltpu.SemaphoreType.DMA],
        compiler_params=pltpu.CompilerParams(vmem_limit_bytes=16 << 20),
        cost_estimate=pl.CostEstimate(
            flops=0, bytes_accessed=4 * stiff.size, transcendentals=0
        ),
    )(stiff)


def class_product(stiff, segment, other_layer, other_core, dtype):
    quarter, _, _, owned, depth = stiff.shape
    members = segment.shape[1]

    def kernel(stiff_ref, segment_ref, out_ref, kept_ref):
        col = lax.axis_index("col")
        layer_parity = (col // 2 + other_layer) % 2
        core = (col + other_core) % 2
        rows = stiff_ref[:, layer_parity, core].reshape(quarter * owned, depth)
        product = jnp.dot(rows, segment_ref[...], preferred_element_type=jnp.float32)
        out_ref[...] = product.reshape(quarter, owned, members).astype(dtype)

    vmem = pl.BlockSpec(memory_space=pltpu.VMEM)
    return pl.pallas_call(
        kernel,
        out_shape=(
            jax.ShapeDtypeStruct((quarter, owned, members), dtype),
            jax.ShapeDtypeStruct(stiff.shape, stiff.dtype),
        ),
        in_specs=[vmem, vmem],
        out_specs=(vmem, vmem),
        input_output_aliases={0: 1},
        compiler_params=pltpu.CompilerParams(vmem_limit_bytes=VMEM_LIMIT),
        cost_estimate=pl.CostEstimate(
            flops=2 * quarter * owned * depth * members,
            bytes_accessed=2 * quarter * owned * depth,
            transcendentals=0,
        ),
    )(stiff, segment)


def dealt(own, received, arrived):
    quarter, owned, members = own.shape

    def kernel(own_ref, received_ref, arrived_ref, *out_refs):
        place = lax.axis_index("col") // 4
        for distance, out_ref in enumerate(out_refs):
            chunk = (place + distance) % quarter
            total = own_ref[chunk] + received_ref[chunk]
            total = total + arrived_ref[chunk].astype(jnp.float32)
            out_ref[...] = total.astype(out_ref.dtype)

    vmem = pl.BlockSpec(memory_space=pltpu.VMEM)
    types = [jnp.float32] + [jnp.bfloat16] * (quarter - 1)
    return pl.pallas_call(
        kernel,
        out_shape=[jax.ShapeDtypeStruct((owned, members), t) for t in types],
        in_specs=[vmem] * 3,
        out_specs=[vmem] * quarter,
        compiler_params=pltpu.CompilerParams(vmem_limit_bytes=VMEM_LIMIT),
    )(own, received, arrived)


def body(
    stiffness, self_stiffness, stress, state, plate_rate, stress_gain, heal_rate, ab_ratio, step
):
    owned, members = stress.shape
    side = lax.axis_size("row")
    layers = side // 2
    row_index = lax.axis_index("row")
    col_index = lax.axis_index("col")
    patch_total = owned * side * side
    params = (self_stiffness, plate_rate, stress_gain, heal_rate, ab_ratio)
    first_patch = (row_index * side + col_index) * owned

    everyone = range(side)
    rows = landing_rows(side, 4)
    spread = [(a * side + b, rows[a][b] * side + a) for a in everyone for b in everyone]
    plane_groups = [[rows[a][b] * side + a for b in everyone] for a in everyone]
    along = [[(c, (c + 4 * d) % side) for c in everyone] for d in range(layers // 2)]
    swap = [(c, c ^ 1) for c in everyone]
    beside = []
    for c in everyone:
        z, core = c // 2, c % 2
        ahead = (z + core) % 2 == 0
        beside.append((c, 2 * ((z + (1 if ahead else -1)) % layers) + core))
    stiff = stiffness.reshape(layers // 2, 2, 2, owned, side * owned)
    positions = first_patch + jnp.arange(owned, dtype=jnp.int32)
    depth = 0.5 + 1.5 * (positions.astype(jnp.float32) + 0.5) / patch_total

    def coupling(sent_block, stiff, late):
        moved = lax.ppermute(sent_block, BOTH, spread)
        copies = jnp.broadcast_to(moved[None], (side, owned, members))
        copies, stiff, late = lax.optimization_barrier((copies, stiff, late))
        segment = lax.all_to_all(
            copies, BOTH, 0, 0, axis_index_groups=plane_groups, tiled=True
        ).reshape(side * owned, members)
        segment, stiff, late = lax.optimization_barrier((segment, stiff, late))
        part, stiff = class_product(stiff, segment, 1, 1, jnp.float32)
        received = lax.ppermute(part, "col", swap)
        own, stiff = class_product(stiff, segment, 1, 0, jnp.float32)
        onward = (own + received.astype(jnp.float32)).astype(jnp.bfloat16)
        arrived = lax.ppermute(onward, "col", beside)
        part, stiff = class_product(stiff, segment, 0, 1, jnp.float32)
        received = lax.ppermute(part, "col", swap)
        own, stiff = class_product(stiff, segment, 0, 0, jnp.float32)
        held, *sent = dealt(own, received, arrived)
        held, sent, stiff, late = lax.optimization_barrier((held, sent, stiff, late))
        coupled = held
        for distance in (2, 1, 3):
            chunk = lax.ppermute(sent[distance - 1], "col", along[distance])
            coupled = coupled + chunk.astype(jnp.float32)
        coupled, stiff, late = lax.optimization_barrier((coupled, stiff, late))
        return coupled, stiff, late

    def section(stress_now, state_now, stiff, late):
        params = late[:5]
        slip_rate, deficit = friction(stress_now, state_now, plate_rate)
        late = (*late, stress_now, state_now)
        coupled, stiff, late = coupling(deficit.astype(jnp.bfloat16), stiff, late)
        *late, stress_now, state_now = late
        slip_rate, deficit = friction(stress_now, state_now, late[1])
        tendencies = rates_from(state_now, slip_rate, deficit, coupled, tuple(late[:5]))
        return tendencies, stiff, tuple(late)

    def total_over(values, axis):
        copies = jnp.broadcast_to(values[None], (side, members))
        return jnp.sum(lax.all_to_all(copies, axis, 0, 0, tiled=True), axis=0)

    depth, stiff = lax.optimization_barrier((depth, stiff))
    late = (*params, step, depth, stress, state)
    (first_u, first_p), stiff, late = section(stress, state, resident(stiff), late)
    *_, step, depth, stress, state = late
    full_step = step[None, :]
    late = (*late, first_u, first_p)
    (second_u, second_p), stiff, late = section(
        stress + full_step * first_u, state + full_step * first_p, stiff, late
    )
    *_, step, depth, stress, state, first_u, first_p = late
    half_step = 0.5 * step[None, :]
    stress_next = stress + half_step * (first_u + second_u)
    state_next = state + half_step * (first_p + second_p)
    squared = (depth[:, None] * half_step * (second_u - first_u)) ** 2 + (
        half_step * (second_p - first_p)
    ) ** 2
    partial_sums = jnp.sum(squared, axis=0)
    summed = total_over(total_over(partial_sums, "col"), "row")
    error_norm = jnp.sqrt(summed / (2 * patch_total) + epsilon) / tolerance
    return (stress_next, state_next, error_norm)


def solution(mesh):
    return jax.shard_map(
        body,
        mesh=mesh,
        in_specs=(
            P("row", "col"),
            P(("row", "col")),
            P(("row", "col"), None),
            P(("row", "col"), None),
            P(("row", "col")),
            P(("row", "col")),
            P(("row", "col")),
            P(("row", "col")),
            P(),
        ),
        out_specs=(P(("row", "col"), None), P(("row", "col"), None), P()),
        check_vma=False,
    )
```
